32 devices in a mesh: grp: 2 (over y), lon: 16 (over z, x, core).
Axes of the slice: x: 2, y: 2, z: 4, core: 2. Of those that a mesh axis runs over, the one named last changes fastest.
Arguments:
- tokens: bfloat16 [256, 32, 512], P(('grp', 'lon')), parts along dimension 0, may hold values from -30 to 30, as said below
- conv_weight: float32 [3, 3, 512], replicated, may hold values from -1.5 to 1.5
- gain_one: float32 [512], replicated, may hold values from 0.1 to 1.9
- gain_two: float32 [512], replicated, may hold values from 0.1 to 1.9
- w_qkv: bfloat16 [512, 1536], replicated, may hold values from -0.25 to 0.25
- rel_bias: float32 [8, 25, 13], replicated, may hold values from -400 to 400
- w_out: bfloat16 [512, 512], replicated, may hold values from -0.25 to 0.25
- w_up: bfloat16 [512, 2048], replicated, may hold values from -0.25 to 0.25
- w_down: bfloat16 [2048, 512], replicated, may hold values from -0.125 to 0.125
Outputs:
- block_out: bfloat16 [256, 32, 512], P(('grp', 'lon')), parts along dimension 0
The draws below stay inside these ranges and needn't reach their ends.
There are 2 independent parts, one for each index of `grp`. The reference program is written for one: setup_inputs(seed, part) draws one part's arguments, and reference() takes and returns one part's arrays. A program takes and returns all parts, laid end to end along the dimension named above; an argument that names none is the same for every part. Nothing has to cross between parts.
Inputs may be any that keep to these rules, and one draw needn't show every extreme that they name: `tokens`: token features of order one.
All inputs are finite; a program needn't handle non-finite values.
Results may differ from the reference program's by a relative error of at most 0.014.
Values may be sent and summed in bfloat16 or wider, within the bound.
A program may use at most 128 MiB of HBM per device.

```python
import jax
import jax.numpy as jnp
from jax import lax

D = 512
HEADS = 8
FF = 2048
WIN = 13
LON_DEV = 8
LAT = 32
LON = 128


def draw_tokens(key, part):
    key_noise = jax.random.fold_in(key, 1)
    field = jnp.clip(jax.random.normal(key_noise, (LON, LAT, D), jnp.float32), -4.0, 4.0)
    return field.astype(jnp.bfloat16)


def draw_rel_bias(key, part):
    key_base = jax.random.fold_in(key, 0)
    base = jnp.clip(jax.random.normal(key_base, (HEADS, 2 * WIN - 1, WIN), jnp.float32), -3.0, 3.0)
    return base.astype(jnp.float32)


def centred(key, extent, scale, bound, kind=jnp.bfloat16):
    array = scale * jax.random.normal(key, extent, jnp.float32)
    return jnp.clip(array, min=-bound, max=bound).astype(kind)


def setup_inputs(seed: int = 0, part: int = 0) -> dict:
    key_of = jax.random.split(jax.random.key(seed), 10)
    own_keys = jax.random.split(jax.random.fold_in(key_of[9], part), 10)
    tokens = draw_tokens(jax.random.fold_in(jax.random.fold_in(key_of[9], part), 71), part)
    conv_weight = centred(key_of[1], (3, 3, D), 0.3, 1.5, jnp.float32)
    gain_one = jnp.clip(1.0 + 0.18 * jax.random.normal(key_of[2], (D,), jnp.float32), 0.1, 1.9)
    gain_two = jnp.clip(1.0 + 0.18 * jax.random.normal(key_of[3], (D,), jnp.float32), 0.1, 1.9)
    w_qkv = centred(key_of[4], (D, 3 * D), D ** -0.5, 0.25)
    rel_bias = draw_rel_bias(jax.random.fold_in(key_of[9], 71), part)
    w_out = centred(key_of[6], (D, D), D ** -0.5, 0.25)
    w_up = centred(key_of[7], (D, FF), D ** -0.5, 0.25)
    w_down = centred(key_of[8], (FF, D), FF ** -0.5, 0.125)
    return dict(tokens=tokens, conv_weight=conv_weight, gain_one=gain_one, gain_two=gain_two, w_qkv=w_qkv, rel_bias=rel_bias, w_out=w_out, w_up=w_up, w_down=w_down)


EPS = 1e-05

def layer_norm(field, gain):
    values = field.astype(jnp.float32)
    center = values - lax.optimization_barrier(jnp.mean(values, axis=-1, keepdims=True))
    spread = lax.optimization_barrier(jnp.mean(center * center, axis=-1, keepdims=True))
    return (center * lax.rsqrt(spread + EPS) * gain).astype(jnp.bfloat16)

def positional(wide, conv_weight):
    columns = wide.shape[0] - 2
    lat_rows = wide.shape[1]
    padded = jnp.pad(wide.astype(jnp.float32), ((0, 0), (1, 1), (0, 0)))
    total = wide[1:-1].astype(jnp.float32)
    for lon_off in range(3):
        for lat_off in range(3):
            total = total + conv_weight[lon_off, lat_off] * padded[lon_off:lon_off + columns, lat_off:lat_off + lat_rows]
    return total.astype(jnp.bfloat16)

def attend(queries, pairs, rel_bias):
    columns, lat_rows, width = queries.shape
    head_count = rel_bias.shape[0]
    window = rel_bias.shape[2]
    radius = (window - 1) // 2
    head_size = width // head_count
    lat_block = 16
    span = lat_block + 2 * radius
    block_count = lat_rows // lat_block
    group = min(4, block_count)
    score_scale = 1.0 / float(head_size) ** 0.5
    padded = jnp.pad(pairs, ((0, 0), (radius, radius), (0, 0)))
    bands = jnp.stack([padded[:, blk * lat_block:blk * lat_block + span] for blk in range(block_count)], axis=1)
    query_blocks = queries.reshape(columns, block_count, lat_block, head_count, head_size)
    firsts = jnp.arange(block_count, dtype=jnp.int32) * lat_block
    key_rows = firsts[:, None] + jnp.arange(span, dtype=jnp.int32)[None, :] - radius
    query_rows = firsts[:, None] + jnp.arange(lat_block, dtype=jnp.int32)[None, :]
    offsets = key_rows[:, None, :] - query_rows[:, :, None]
    table = jnp.clip(offsets + window - 1, 0, 2 * window - 2)
    bias_all = jnp.transpose(rel_bias[:, table, :], (1, 0, 2, 4, 3)).reshape(block_count, head_count, lat_block, window * span)
    starts = jnp.clip(query_rows - radius, 0, lat_rows - window)
    valid_all = (key_rows[:, None, :] >= starts[:, :, None]) & (key_rows[:, None, :] < starts[:, :, None] + window)
    valid_all = jnp.tile(valid_all, (1, 1, window))

    def one_group(index):
        first = (index * group).astype(jnp.int32)
        block_q = lax.dynamic_slice_in_dim(query_blocks, first, group, 1).astype(jnp.float32)
        block_kv = lax.dynamic_slice_in_dim(bands, first, group, 1)
        bias = lax.dynamic_slice_in_dim(bias_all, first, group, 0)
        valid = lax.dynamic_slice_in_dim(valid_all, first, group, 0)
        parts = []
        for offset in range(window):
            keys = block_kv[offset:offset + columns, ..., :width].reshape(columns, group, span, head_count, head_size).astype(jnp.float32)
            parts.append(jnp.einsum('cnqhe,cnkhe->cnhqk', block_q, keys))
        scores = jnp.concatenate(parts, axis=-1) * score_scale
        scores = scores + bias[None]
        scores = jnp.where(valid[None, :, None], scores, -1e+30)
        top = lax.optimization_barrier(jnp.max(scores, axis=-1, keepdims=True))
        expo = jnp.exp(scores - top)
        weights = (expo / lax.optimization_barrier(jnp.sum(expo, axis=-1, keepdims=True))).astype(jnp.bfloat16).astype(jnp.float32)
        total = jnp.zeros((columns, group, lat_block, head_count, head_size), jnp.float32)
        for offset in range(window):
            values = block_kv[offset:offset + columns, ..., width:].reshape(columns, group, span, head_count, head_size).astype(jnp.float32)
            total = total + jnp.einsum('cnhqk,cnkhe->cnqhe', weights[..., offset * span:(offset + 1) * span], values)
        return total.astype(jnp.bfloat16).reshape(columns, group * lat_block, width)
    blocks = lax.map(one_group, jnp.arange(block_count // group, dtype=jnp.int32))
    return jnp.moveaxis(blocks, 0, 1).reshape(columns, lat_rows, width)

def finish(mixed_in, attended, gain_two, w_out, w_up, w_down):
    width = mixed_in.shape[-1]
    flat_in = mixed_in.reshape(-1, width)
    stream = (flat_in.astype(jnp.float32) + jnp.dot(attended.reshape(-1, width), w_out, preferred_element_type=jnp.float32)).astype(jnp.bfloat16)
    normed = layer_norm(stream, gain_two)
    hidden = jax.nn.gelu(jnp.dot(normed, w_up, preferred_element_type=jnp.float32)).astype(jnp.bfloat16)
    result = stream.astype(jnp.float32) + jnp.dot(hidden, w_down, preferred_element_type=jnp.float32)
    return result.astype(jnp.bfloat16).reshape(mixed_in.shape)

def reference(tokens, conv_weight, gain_one, gain_two, w_qkv, rel_bias, w_out, w_up, w_down):
    total_cols, lat_rows, width = tokens.shape
    radius = (WIN - 1) // 2
    wide = jnp.concatenate([tokens[-1:], tokens, tokens[:1]], axis=0)
    mixed_in = positional(wide, conv_weight)
    normed = layer_norm(mixed_in, gain_one).reshape(-1, width)
    queries = jnp.dot(normed, w_qkv[:, :width], preferred_element_type=jnp.float32).astype(jnp.bfloat16).reshape(total_cols, lat_rows, width)
    pairs = jnp.dot(normed, w_qkv[:, width:], preferred_element_type=jnp.float32).astype(jnp.bfloat16).reshape(total_cols, lat_rows, 2 * width)
    pairs_wide = jnp.concatenate([pairs[-radius:], pairs, pairs[:radius]], axis=0)

    def member(index):
        first = (index * LON_DEV).astype(jnp.int32)
        zero = jnp.int32(0)
        part_q = lax.dynamic_slice(queries, (first, zero, zero), (LON_DEV, lat_rows, width))
        part_kv = lax.dynamic_slice(pairs_wide, (first, zero, zero), (LON_DEV + 2 * radius, lat_rows, 2 * width))
        return attend(part_q, part_kv, rel_bias)
    attended = lax.map(member, jnp.arange(total_cols // LON_DEV, dtype=jnp.int32)).reshape(total_cols, lat_rows, width)
    return finish(mixed_in, attended, gain_two, w_out, w_up, w_down)
```

```python
import functools

import jax
import jax.numpy as jnp
from jax import lax
from jax.experimental import pallas as pl
from jax.experimental.pallas import tpu as pltpu
from jax.sharding import PartitionSpec as P

EPS = 1e-05
F32 = jnp.float32
BF16 = jnp.bfloat16
MASKED = -1e30


def norm(values, gain):
    center = values - jnp.mean(values, axis=-1, keepdims=True)
    spread = jnp.mean(center * center, axis=-1, keepdims=True)
    return (center * lax.rsqrt(spread + EPS) * gain).astype(BF16)


def gelu(x):
    half = x * BF16(0.5)
    inner = x * (BF16(0.7978845608028654) + BF16(0.035677408136300125) * (x * x))
    return half + half * jnp.tanh(inner)


def block_kernel(
    dims,
    tok_ref,
    conv_hbm,
    gain_one_hbm,
    gain_two_hbm,
    w_qkv_ref,
    bias_hbm,
    w_out_ref,
    w_up_ref,
    w_down_ref,
    out_ref,
    wide,
    normed,
    mixed,
    q_t,
    k_s,
    v_t,
    att_t,
    bias_s,
    w_qt,
    w_vt,
    score_s,
    prob_s,
    top_s,
    sum_s,
    held,
    w_qkv,
    w_out,
    w_up,
    w_down,
    conv_ref,
    gain_one_ref,
    gain_two_ref,
    bias_ref,
    load_sem,
    send_sem,
    recv_sem,
):
    columns, lat, width, heads, window, ff = dims
    radius = (window - 1) // 2
    reach = radius + 1
    keys = columns + 2 * radius
    head = width // heads
    tile = 128 // lat
    span = (columns + 2 * radius - tile) * lat
    pairs = heads // 2
    near = reach - tile
    groups = keys // tile
    axis = lax.axis_size("lon")
    me = lax.axis_index("lon")
    east, west = lax.rem(me + 1, axis), lax.rem(me + axis - 1, axis)
    core = lax.rem(me, 2)
    odd = jnp.where(me == 1, 0, core)

    barrier = pltpu.get_barrier_semaphore()
    for neighbour in (west, east):
        pl.semaphore_signal(
            barrier, inc=1, device_id={"lon": neighbour}, device_id_type=pl.DeviceIdType.MESH
        )
    loads = [
        pltpu.make_async_copy(tok_ref, wide.at[reach : reach + columns], load_sem.at[0]),
        pltpu.make_async_copy(w_qkv_ref, w_qkv, load_sem.at[1]),
        pltpu.make_async_copy(w_out_ref, w_out, load_sem.at[2]),
        pltpu.make_async_copy(w_up_ref, w_up, load_sem.at[3]),
        pltpu.make_async_copy(w_down_ref, w_down, load_sem.at[4]),
        pltpu.make_async_copy(conv_hbm, conv_ref, load_sem.at[5]),
        pltpu.make_async_copy(gain_one_hbm, gain_one_ref, load_sem.at[6]),
        pltpu.make_async_copy(gain_two_hbm, gain_two_ref, load_sem.at[7]),
        pltpu.make_async_copy(bias_hbm, bias_ref, load_sem.at[8]),
    ]
    for at in (8, 0, 5, 6, 7, 1, 2, 3, 4):
        loads[at].start()
    spans = (
        (east, columns - near, reach - near, near),
        (west, 0, reach + columns, near),
        (east, columns - reach, 0, reach - near),
        (west, near, reach + columns + near, reach - near),
    )
    sends = [
        pltpu.make_async_remote_copy(
            src_ref=tok_ref.at[source : source + size],
            dst_ref=wide.at[target : target + size],
            send_sem=send_sem.at[at],
            recv_sem=recv_sem.at[at],
            device_id={"lon": who},
            device_id_type=pl.DeviceIdType.MESH,
        )
        for at, (who, source, target, size) in enumerate(spans)
    ]
    first = me == 0
    second = jnp.logical_and(core == 1, me != axis - 1)

    def exchange(now):
        @pl.when(now)
        def _():
            pl.semaphore_wait(barrier, 2)
            for send in sends:
                send.start()

    exchange(jnp.logical_not(jnp.logical_or(first, second)))

    def arrive(far, side):
        start = side * (columns + reach + (0 if not far else near)) + (1 - side) * (
            0 if far else reach - near
        )
        size = reach - near if far else near
        pltpu.make_async_remote_copy(
            src_ref=tok_ref.at[0:size],
            dst_ref=wide.at[pl.ds(start, size)],
            send_sem=send_sem.at[2 * far + side],
            recv_sem=recv_sem.at[2 * far + side],
            device_id={"lon": east},
            device_id_type=pl.DeviceIdType.MESH,
        ).wait_recv()

    offsets = 2 * window - 1
    loads[8].wait()
    row = lax.broadcasted_iota(jnp.int32, (128, 128), 0)
    lane = lax.broadcasted_iota(jnp.int32, (128, 128), 1)
    flip = ((lane == (window - 1 - row + 128) % 128) & (row < offsets)).astype(F32)
    turned = []
    for b in range(window):
        piece = jnp.concatenate([bias_ref[b], jnp.zeros((heads, 128 - offsets), F32)], axis=1)
        turned.append(
            jnp.dot(
                piece, flip, preferred_element_type=F32, precision=lax.Precision.HIGHEST
            )
        )
    key_row = lax.broadcasted_iota(jnp.int32, (lat, 128), 0)
    lane = lax.broadcasted_iota(jnp.int32, (lat, 128), 1)
    lane_column = lane // lat
    start = jnp.clip(lane % lat - radius, 0, lat - window)
    inside = (key_row >= start) & (key_row < start + window)
    for kk in range(span // lat):
        line = jnp.zeros((heads, 128), F32)
        for cc in range(tile):
            if 0 <= kk - cc < window:
                line = line + pltpu.roll(turned[kk - cc], cc * lat, 1)
        valid = inside & (lane_column <= kk) & (lane_column > kk - window)
        for h in range(heads):
            spread = jnp.broadcast_to(line[h : h + 1], (lat, 128))
            rolled = pltpu.roll(spread, 0, 1, stride=1, stride_axis=0)
            bias_s[h // 2, kk * lat : (kk + 1) * lat, (h % 2) * 128 : (h % 2 + 1) * 128] = (
                jnp.where(valid, rolled, MASKED)
            )

    exchange(second)
    rows = lax.broadcasted_iota(jnp.int32, (lat, width), 0)

    def mix(first, count):
        gain_one = gain_one_ref[...]
        for m in range(first, first + count):
            j = m + odd * (keys - 1 - 2 * m)
            x = [wide[j + p].astype(F32) for p in range(3)]
            y = [
                conv_ref[0, q : q + 1] * x[0]
                + conv_ref[1, q : q + 1] * x[1]
                + conv_ref[2, q : q + 1] * x[2]
                for q in range(3)
            ]
            above = jnp.where(rows == 0, 0.0, pltpu.roll(y[0], 1, 0))
            below = jnp.where(rows == lat - 1, 0.0, pltpu.roll(y[2], lat - 1, 0))
            total = ((x[1] + y[1]) + (above + below)).astype(BF16)
            mixed[j] = total
            normed[j] = norm(total.astype(F32), gain_one)

    def project(m):
        g = m + odd * (groups - 1 - 2 * m)
        flat = normed[pl.ds(g * tile, tile)].reshape(128, width)
        at = pl.ds(pl.multiple_of(g * 128, 128), 128)
        k_s[at] = jnp.dot(
            flat, w_qkv[:, width : 2 * width], preferred_element_type=F32
        ).astype(BF16)
        v_t[:, at] = lax.dot_general(
            w_vt[...], flat, (((1,), (1,)), ((), ())), preferred_element_type=F32
        ).astype(BF16)

    scale = 1.0 / float(head) ** 0.5

    def tile_of(late):
        return odd if late else 1 - odd

    def query(late):
        first = radius + tile_of(late) * tile
        q_t[late] = (
            lax.dot_general(
                w_qt[...],
                normed[pl.ds(first, tile)].reshape(128, width),
                (((1,), (1,)), ((), ())),
                preferred_element_type=F32,
            ).astype(BF16)
            * scale
        ).astype(BF16)

    blank = jnp.zeros((head, 128), BF16)
    early = span - 128

    def place(block):
        late, part, pair = block
        size = 128 if part else early
        off = odd * early if part else (1 - odd) * 128
        there = pl.ds(pl.multiple_of(tile_of(late) * 128 + off, 128), size)
        return size, pl.ds(pl.multiple_of(off, 128), size), there, slice(pair * 2 * head, (pair + 1) * 2 * head)

    def score(step, block):
        late, part, pair = block
        size, off, there, at = place(block)
        q_a = q_t[late, pair * 2 * head : pair * 2 * head + head]
        q_b = q_t[late, pair * 2 * head + head : (pair + 1) * 2 * head]
        q_two = jnp.concatenate(
            [jnp.concatenate([q_a, blank], axis=1), jnp.concatenate([blank, q_b], axis=1)],
            axis=0,
        )
        scores = jnp.dot(k_s[there, at], q_two, preferred_element_type=F32) + bias_s[pair, off]
        score_s[step % 2, :size] = scores
        top = jnp.max(scores, axis=0, keepdims=True)
        if part:
            top = jnp.maximum(top, top_s[late, pair])
        else:
            top_s[late, pair] = top
        return top

    def soften(step, block, top):
        size = place(block)[0]
        expo = jnp.exp(score_s[step % 2, :size] - top)
        prob_s[step % 2, :size] = expo.astype(BF16)
        return jnp.sum(expo, axis=0, keepdims=True)

    def gather(step, block, top, total):
        late, part, pair = block
        size, _, there, at = place(block)
        o = jnp.dot(v_t[at, there], prob_s[step % 2, :size], preferred_element_type=F32)
        o_a, o_b = o[:head, :128], o[head:, 128:]
        if part:
            keep = jnp.exp(top_s[late, pair] - top)
            scaled = 1.0 / (total + keep * sum_s[late, pair])
            keep = keep * scaled
            o_a = o_a * scaled[:, :128] + held[late, pair, :head] * keep[:, :128]
            o_b = o_b * scaled[:, 128:] + held[late, pair, head:] * keep[:, 128:]
            att_t[tile_of(late), at] = jnp.concatenate([o_a, o_b], axis=0).astype(BF16)
        else:
            sum_s[late, pair] = total
            held[late, pair] = jnp.concatenate([o_a, o_b], axis=0)

    def attend(blocks):
        tops, sums = {}, {}
        for step in range(len(blocks) + 2):
            if step < len(blocks):
                tops[step] = score(step, blocks[step])
            if 0 <= step - 1 < len(blocks):
                sums[step - 1] = soften(step - 1, blocks[step - 1], tops[step - 1])
            if 0 <= step - 2 < len(blocks):
                gather(step - 2, blocks[step - 2], tops[step - 2], sums[step - 2])

    for at in (0, 5, 6, 7):
        loads[at].wait()
    mix(reach, columns - 2)
    loads[1].wait()
    w_qt[...] = w_qkv[:, :width].T
    w_vt[...] = w_qkv[:, 2 * width : 3 * width].T
    project(2)
    exchange(first)
    arrive(0, 1 - odd)
    mix(keys - reach, near)
    project(3)
    query(0)
    arrive(1, 1 - odd)
    mix(keys - tile, tile)
    project(4)
    attend([(0, 0, pair) for pair in range(pairs)])
    arrive(0, odd)
    mix(tile, near)
    query(1)
    project(1)
    attend([(0, 1, pair) for pair in range(pairs)] + [(1, 0, pair) for pair in range(pairs)])
    for at in (2, 3, 4):
        loads[at].wait()
    arrive(1, odd)
    mix(0, tile)
    project(0)
    attend([(1, 1, pair) for pair in range(pairs)])

    flat_in = mixed[radius : radius + columns].reshape(columns * lat, width)
    attended = jnp.concatenate([att_t[t] for t in range(columns // tile)], axis=1)
    stream = (
        flat_in.astype(F32) + lax.dot_general(
            attended, w_out[...], (((0,), (0,)), ((), ())), preferred_element_type=F32
        )
    ).astype(BF16)
    normed_two = norm(stream.astype(F32), gain_two_ref[...])
    total = stream.astype(F32)
    chunk = 512

    def raise_(at):
        return jnp.dot(normed_two, w_up[:, at : at + chunk], preferred_element_type=F32)

    ahead = raise_(0)
    for at in range(0, ff, chunk):
        now = ahead
        if at + chunk < ff:
            ahead = raise_(at + chunk)
        hidden = gelu(now.astype(BF16))
        total = total + jnp.dot(hidden, w_down[at : at + chunk], preferred_element_type=F32)
    out_ref[...] = total.astype(BF16).reshape(columns, lat, width)
    for send in sends:
        send.wait_send()


def on_device(tokens, conv_weight, gain_one, gain_two, w_qkv, rel_bias, w_out, w_up, w_down):
    columns, lat, width = tokens.shape
    heads, _, window = rel_bias.shape
    ff = w_up.shape[1]
    radius = (window - 1) // 2
    keys = columns + 2 * radius
    dims = (columns, lat, width, heads, window, ff)
    vmem = pl.BlockSpec(memory_space=pltpu.VMEM)
    hbm = pl.BlockSpec(memory_space=pltpu.MemorySpace.HBM)
    return pl.pallas_call(
        functools.partial(block_kernel, dims),
        out_shape=pltpu.VMEM(tokens.shape, BF16),
        in_specs=[hbm] * 9,
        out_specs=vmem,
        scratch_shapes=[
            pltpu.VMEM((keys + 2, lat, width), BF16),
            pltpu.VMEM((keys, lat, width), BF16),
            pltpu.VMEM((keys, lat, width), BF16),
            pltpu.VMEM((2, width, 128), BF16),
            pltpu.VMEM((keys * lat, width), BF16),
            pltpu.VMEM((width, keys * lat), BF16),
            pltpu.VMEM((2, width, 128), BF16),
            pltpu.VMEM((heads // 2, keys * lat - 128, 256), F32),
            pltpu.VMEM((width, width), BF16),
            pltpu.VMEM((width, width), BF16),
            pltpu.VMEM((2, keys * lat - 128, 256), F32),
            pltpu.VMEM((2, keys * lat - 128, 256), BF16),
            pltpu.VMEM((2, heads // 2, 1, 256), F32),
            pltpu.VMEM((2, heads // 2, 1, 256), F32),
            pltpu.VMEM((2, heads // 2, 2 * width // heads, 128), F32),
            pltpu.VMEM(w_qkv.shape, BF16),
            pltpu.VMEM(w_out.shape, BF16),
            pltpu.VMEM(w_up.shape, BF16),
            pltpu.VMEM(w_down.shape, BF16),
            pltpu.VMEM(conv_weight.shape, F32),
            pltpu.VMEM((1, width), F32),
            pltpu.VMEM((1, width), F32),
            pltpu.VMEM((window, heads, rel_bias.shape[1]), F32),
            pltpu.SemaphoreType.DMA((9,)),
            pltpu.SemaphoreType.DMA((4,)),
            pltpu.SemaphoreType.DMA((4,)),
        ],
        compiler_params=pltpu.CompilerParams(
            collective_id=0, has_side_effects=True, vmem_limit_bytes=64 * 1024 * 1024 - 327680
        ),
    )(
        tokens,
        conv_weight,
        gain_one.reshape(1, width),
        gain_two.reshape(1, width),
        w_qkv,
        jnp.transpose(rel_bias, (2, 0, 1)),
        w_out,
        w_up,
        w_down,
    )


def solution(mesh):
    placed = (P(("grp", "lon"), None, None), P(), P(), P(), P(), P(), P(), P(), P())
    return jax.shard_map(
        on_device,
        mesh=mesh,
        in_specs=placed,
        out_specs=P(("grp", "lon"), None, None),
        check_vma=False,
    )
```

```python
import functools

import jax
import jax.numpy as jnp
from jax import lax
from jax.experimental import pallas as pl
from jax.experimental.pallas import tpu as pltpu
from jax.sharding import PartitionSpec as P

EPS = 1e-05
LOG2E = 1.4426950408889634
F32 = jnp.float32
BF16 = jnp.bfloat16
MASKED = -1e30


def norm(values, gain):
    center = values - jnp.mean(values, axis=-1, keepdims=True)
    spread = jnp.mean(center * center, axis=-1, keepdims=True)
    return (center * lax.rsqrt(spread + EPS) * gain).astype(BF16)


def gelu(x):
    half = x * BF16(0.5)
    inner = x * (BF16(0.7978845608028654) + BF16(0.035677408136300125) * (x * x))
    return half + half * jnp.tanh(inner)


def block_kernel(
    dims,
    tok_ref,
    conv_hbm,
    gain_one_hbm,
    gain_two_hbm,
    w_qkv_ref,
    bias_hbm,
    w_out_ref,
    w_up_ref,
    w_down_ref,
    out_ref,
    wide,
    normed,
    mixed,
    q_t,
    k_s,
    v_t,
    att_t,
    bias_s,
    w_qt,
    w_vt,
    score_s,
    prob_s,
    top_s,
    sum_s,
    held,
    w_qkv,
    w_out,
    w_up,
    w_down,
    conv_ref,
    gain_one_ref,
    gain_two_ref,
    bias_ref,
    load_sem,
    send_sem,
    recv_sem,
):
    columns, lat, width, heads, window, ff = dims
    radius = (window - 1) // 2
    reach = radius + 1
    keys = columns + 2 * radius
    head = width // heads
    tile = 128 // lat
    span = (columns + 2 * radius - tile) * lat
    pairs = heads // 2
    near = reach - tile
    groups = keys // tile
    axis = lax.axis_size("lon")
    me = lax.axis_index("lon")
    east, west = lax.rem(me + 1, axis), lax.rem(me + axis - 1, axis)
    core = lax.rem(me, 2)
    odd = jnp.where(me == 1, 0, core)

    barrier = pltpu.get_barrier_semaphore()
    for neighbour in (west, east):
        pl.semaphore_signal(
            barrier, inc=1, device_id={"lon": neighbour}, device_id_type=pl.DeviceIdType.MESH
        )
    loads = [
        pltpu.make_async_copy(tok_ref, wide.at[reach : reach + columns], load_sem.at[0]),
        pltpu.make_async_copy(w_qkv_ref, w_qkv, load_sem.at[1]),
        pltpu.make_async_copy(w_out_ref, w_out, load_sem.at[2]),
        pltpu.make_async_copy(w_up_ref, w_up, load_sem.at[3]),
        pltpu.make_async_copy(w_down_ref, w_down, load_sem.at[4]),
        pltpu.make_async_copy(conv_hbm, conv_ref, load_sem.at[5]),
        pltpu.make_async_copy(gain_one_hbm, gain_one_ref, load_sem.at[6]),
        pltpu.make_async_copy(gain_two_hbm, gain_two_ref, load_sem.at[7]),
        pltpu.make_async_copy(bias_hbm, bias_ref, load_sem.at[8]),
    ]
    for at in (8, 0, 5, 6, 7, 1, 2, 3, 4):
        loads[at].start()
    spans = (
        (east, columns - near, reach - near, near),
        (west, 0, reach + columns, near),
        (east, columns - reach, 0, reach - near),
        (west, near, reach + columns + near, reach - near),
    )
    sends = [
        pltpu.make_async_remote_copy(
            src_ref=tok_ref.at[source : source + size],
            dst_ref=wide.at[target : target + size],
            send_sem=send_sem.at[at],
            recv_sem=recv_sem.at[at],
            device_id={"lon": who},
            device_id_type=pl.DeviceIdType.MESH,
        )
        for at, (who, source, target, size) in enumerate(spans)
    ]
    first = me == 0
    second = jnp.logical_and(core == 1, me != axis - 1)

    def exchange(now):
        @pl.when(now)
        def _():
            pl.semaphore_wait(barrier, 2)
            for send in sends:
                send.start()

    exchange(jnp.logical_not(jnp.logical_or(first, second)))

    def arrive(far, side):
        start = side * (columns + reach + (0 if not far else near)) + (1 - side) * (
            0 if far else reach - near
        )
        size = reach - near if far else near
        pltpu.make_async_remote_copy(
            src_ref=tok_ref.at[0:size],
            dst_ref=wide.at[pl.ds(start, size)],
            send_sem=send_sem.at[2 * far + side],
            recv_sem=recv_sem.at[2 * far + side],
            device_id={"lon": east},
            device_id_type=pl.DeviceIdType.MESH,
        ).wait_recv()

    offsets = 2 * window - 1
    loads[8].wait()
    row = lax.broadcasted_iota(jnp.int32, (128, 128), 0)
    lane = lax.broadcasted_iota(jnp.int32, (128, 128), 1)
    flip = ((lane == (window - 1 - row + 128) % 128) & (row < offsets)).astype(F32)
    turned = []
    for b in range(window):
        piece = jnp.concatenate([bias_ref[b], jnp.zeros((heads, 128 - offsets), F32)], axis=1)
        turned.append(
            jnp.dot(
                piece, flip, preferred_element_type=F32, precision=lax.Precision.HIGHEST
            )
            * LOG2E
        )
    key_row = lax.broadcasted_iota(jnp.int32, (lat, 128), 0)
    lane = lax.broadcasted_iota(jnp.int32, (lat, 128), 1)
    lane_column = lane // lat
    start = jnp.clip(lane % lat - radius, 0, lat - window)
    inside = (key_row >= start) & (key_row < start + window)
    for kk in range(span // lat):
        line = jnp.zeros((heads, 128), F32)
        for cc in range(tile):
            if 0 <= kk - cc < window:
                line = line + pltpu.roll(turned[kk - cc], cc * lat, 1)
        valid = inside & (lane_column <= kk) & (lane_column > kk - window)
        for h in range(heads):
            spread = jnp.broadcast_to(line[h : h + 1], (lat, 128))
            rolled = pltpu.roll(spread, 0, 1, stride=1, stride_axis=0)
            bias_s[h // 2, kk * lat : (kk + 1) * lat, (h % 2) * 128 : (h % 2 + 1) * 128] = (
                jnp.where(valid, rolled, MASKED)
            )

    exchange(second)
    rows = lax.broadcasted_iota(jnp.int32, (lat, width), 0)

    def mix(first, count):
        gain_one = gain_one_ref[...]
        taps = [conv_ref[r + odd * (2 - 2 * r)] for r in range(3)]
        taps[1] = taps[1] + (lax.broadcasted_iota(jnp.int32, (3, width), 0) == 1).astype(F32)

        def fetch(u):
            return wide[u + odd * (keys + 1 - 2 * u)].astype(F32)

        x = [fetch(first), fetch(first + 1)]
        for m in range(first, first + count):
            j = m + odd * (keys - 1 - 2 * m)
            x = x[-2:] + [fetch(m + 2)]
            y = [
                taps[0][q : q + 1] * x[0] + taps[1][q : q + 1] * x[1] + taps[2][q : q + 1] * x[2]
                for q in range(3)
            ]
            above = pltpu.roll(y[0], 1, 0)
            above = jnp.concatenate([jnp.where(rows[:8] == 0, 0.0, above[:8]), above[8:]], axis=0)
            below = pltpu.roll(y[2], lat - 1, 0)
            below = jnp.concatenate(
                [below[: lat - 8], jnp.where(rows[lat - 8 :] == lat - 1, 0.0, below[lat - 8 :])], axis=0
            )
            total = (y[1] + (above + below)).astype(BF16)
            mixed[j] = total
            normed[j] = norm(total.astype(F32), gain_one)

    def project(m):
        g = m + odd * (groups - 1 - 2 * m)
        flat = normed[pl.ds(g * tile, tile)].reshape(128, width)
        at = pl.ds(pl.multiple_of(g * 128, 128), 128)
        k_s[at] = jnp.dot(
            flat, w_qkv[:, width : 2 * width], preferred_element_type=F32
        ).astype(BF16)
        v_t[:, at] = lax.dot_general(
            w_vt[...], flat, (((1,), (1,)), ((), ())), preferred_element_type=F32
        ).astype(BF16)

    scale = LOG2E / float(head) ** 0.5

    def tile_of(late):
        return odd if late else 1 - odd

    def query(late):
        first = radius + tile_of(late) * tile
        q_t[late] = (
            lax.dot_general(
                w_qt[...],
                normed[pl.ds(first, tile)].reshape(128, width),
                (((1,), (1,)), ((), ())),
                preferred_element_type=F32,
            )
            * scale
        ).astype(BF16)

    blank = jnp.zeros((head, 128), BF16)
    early = span - 128

    def place(block):
        late, part, pair = block
        size = 128 if part else early
        off = odd * early if part else (1 - odd) * 128
        there = pl.ds(pl.multiple_of(tile_of(late) * 128 + off, 128), size)
        return size, pl.ds(pl.multiple_of(off, 128), size), there, slice(pair * 2 * head, (pair + 1) * 2 * head)

    def score(step, block):
        late, part, pair = block
        size, off, there, at = place(block)
        q_a = q_t[late, pair * 2 * head : pair * 2 * head + head]
        q_b = q_t[late, pair * 2 * head + head : (pair + 1) * 2 * head]
        q_two = jnp.concatenate(
            [jnp.concatenate([q_a, blank], axis=1), jnp.concatenate([blank, q_b], axis=1)],
            axis=0,
        )
        scores = jnp.dot(k_s[there, at], q_two, preferred_element_type=F32) + bias_s[pair, off]
        score_s[step % 2, :size] = scores
        top = jnp.max(scores, axis=0, keepdims=True)
        if part:
            top = jnp.maximum(top, top_s[late, pair])
        else:
            top_s[late, pair] = top
        return top

    def soften(step, block, top):
        size = place(block)[0]
        prob_s[step % 2, :size] = jnp.exp2((score_s[step % 2, :size] - top).astype(BF16))

    def gather(step, block, top):
        late, part, pair = block
        size, _, there, at = place(block)
        o = jnp.dot(v_t[at, there], prob_s[step % 2, :size], preferred_element_type=F32)
        total = jnp.dot(
            jnp.ones((16, size), BF16), prob_s[step % 2, :size], preferred_element_type=F32
        )[:1]
        o_a, o_b = o[:head, :128], o[head:, 128:]
        if part:
            keep = jnp.exp2(top_s[late, pair] - top)
            scaled = 1.0 / (total + keep * sum_s[late, pair])
            keep = keep * scaled
            o_a = o_a * scaled[:, :128] + held[late, pair, :head] * keep[:, :128]
            o_b = o_b * scaled[:, 128:] + held[late, pair, head:] * keep[:, 128:]
            att_t[tile_of(late), at] = jnp.concatenate([o_a, o_b], axis=0).astype(BF16)
        else:
            sum_s[late, pair] = total
            held[late, pair] = jnp.concatenate([o_a, o_b], axis=0)

    def attend(blocks):
        tops = {}
        for step in range(len(blocks) + 2):
            if step < len(blocks):
                tops[step] = score(step, blocks[step])
            if 0 <= step - 1 < len(blocks):
                soften(step - 1, blocks[step - 1], tops[step - 1])
            if 0 <= step - 2 < len(blocks):
                gather(step - 2, blocks[step - 2], tops[step - 2])

    for at in (0, 5, 6, 7):
        loads[at].wait()
    mix(reach, columns - 2)
    loads[1].wait()
    w_qt[...] = w_qkv[:, :width].T
    w_vt[...] = w_qkv[:, 2 * width : 3 * width].T
    project(2)
    arrive(0, 1 - odd)
    mix(keys - reach, near)
    project(3)
    query(0)
    exchange(first)
    arrive(1, 1 - odd)
    mix(keys - tile, tile)
    project(4)
    attend([(0, 0, pair) for pair in range(pairs)])
    arrive(0, odd)
    mix(tile, near)
    query(1)
    project(1)
    attend([(0, 1, pair) for pair in range(pairs)] + [(1, 0, pair) for pair in range(pairs)])
    for at in (2, 3, 4):
        loads[at].wait()
    arrive(1, odd)
    mix(0, tile)
    project(0)
    attend([(1, 1, pair) for pair in range(pairs)])

    flat_in = mixed[radius : radius + columns].reshape(columns * lat, width)
    attended = jnp.concatenate([att_t[t] for t in range(columns // tile)], axis=1)
    stream = (
        flat_in.astype(F32) + lax.dot_general(
            attended, w_out[...], (((0,), (0,)), ((), ())), preferred_element_type=F32
        )
    ).astype(BF16)
    normed_two = norm(stream.astype(F32), gain_two_ref[...])
    total = stream.astype(F32)
    chunk = 512

    def raise_(at):
        return jnp.dot(normed_two, w_up[:, at : at + chunk], preferred_element_type=F32)

    ahead = raise_(0)
    for at in range(0, ff, chunk):
        now = ahead
        if at + chunk < ff:
            ahead = raise_(at + chunk)
        hidden = gelu(now.astype(BF16))
        total = total + jnp.dot(hidden, w_down[at : at + chunk], preferred_element_type=F32)
    out_ref[...] = total.astype(BF16).reshape(columns, lat, width)
    for send in sends:
        send.wait_send()


def on_device(tokens, conv_weight, gain_one, gain_two, w_qkv, rel_bias, w_out, w_up, w_down):
    columns, lat, width = tokens.shape
    heads, _, window = rel_bias.shape
    ff = w_up.shape[1]
    radius = (window - 1) // 2
    keys = columns + 2 * radius
    dims = (columns, lat, width, heads, window, ff)
    vmem = pl.BlockSpec(memory_space=pltpu.VMEM)
    hbm = pl.BlockSpec(memory_space=pltpu.MemorySpace.HBM)
    return pl.pallas_call(
        functools.partial(block_kernel, dims),
        out_shape=pltpu.VMEM(tokens.shape, BF16),
        in_specs=[hbm] * 9,
        out_specs=vmem,
        scratch_shapes=[
            pltpu.VMEM((keys + 2, lat, width), BF16),
            pltpu.VMEM((keys, lat, width), BF16),
            pltpu.VMEM((keys, lat, width), BF16),
            pltpu.VMEM((2, width, 128), BF16),
            pltpu.VMEM((keys * lat, width), BF16),
            pltpu.VMEM((width, keys * lat), BF16),
            pltpu.VMEM((2, width, 128), BF16),
            pltpu.VMEM((heads // 2, keys * lat - 128, 256), F32),
            pltpu.VMEM((width, width), BF16),
            pltpu.VMEM((width, width), BF16),
            pltpu.VMEM((2, keys * lat - 128, 256), F32),
            pltpu.VMEM((2, keys * lat - 128, 256), BF16),
            pltpu.VMEM((2, heads // 2, 1, 256), F32),
            pltpu.VMEM((2, heads // 2, 1, 256), F32),
            pltpu.VMEM((2, heads // 2, 2 * width // heads, 128), F32),
            pltpu.VMEM(w_qkv.shape, BF16),
            pltpu.VMEM(w_out.shape, BF16),
            pltpu.VMEM(w_up.shape, BF16),
            pltpu.VMEM(w_down.shape, BF16),
            pltpu.VMEM(conv_weight.shape, F32),
            pltpu.VMEM((1, width), F32),
            pltpu.VMEM((1, width), F32),
            pltpu.VMEM((window, heads, rel_bias.shape[1]), F32),
            pltpu.SemaphoreType.DMA((9,)),
            pltpu.SemaphoreType.DMA((4,)),
            pltpu.SemaphoreType.DMA((4,)),
        ],
        compiler_params=pltpu.CompilerParams(
            collective_id=0, has_side_effects=True, vmem_limit_bytes=64 * 1024 * 1024 - 327680
        ),
    )(
        tokens,
        conv_weight,
        gain_one.reshape(1, width),
        gain_two.reshape(1, width),
        w_qkv,
        jnp.transpose(rel_bias, (2, 0, 1)),
        w_out,
        w_up,
        w_down,
    )


def solution(mesh):
    placed = (P(("grp", "lon"), None, None), P(), P(), P(), P(), P(), P(), P(), P())
    return jax.shard_map(
        on_device,
        mesh=mesh,
        in_specs=placed,
        out_specs=P(("grp", "lon"), None, None),
        check_vma=False,
    )
```

```python
import functools

import jax
import jax.numpy as jnp
from jax import lax
from jax.experimental import pallas as pl
from jax.experimental.pallas import tpu as pltpu
from jax.sharding import PartitionSpec as P

EPS = 1e-05
LOG2E = 1.4426950408889634
F32 = jnp.float32
BF16 = jnp.bfloat16
MASKED = -1e30


def norm(values, gain):
    center = values - jnp.mean(values, axis=-1, keepdims=True)
    spread = jnp.mean(center * center, axis=-1, keepdims=True)
    return (center * lax.rsqrt(spread + EPS) * gain).astype(BF16)


def gelu(x):
    half = x * BF16(0.5)
    inner = x * (BF16(0.7978845608028654) + BF16(0.035677408136300125) * (x * x))
    return half + half * jnp.tanh(inner)


def block_kernel(
    dims,
    tok_ref,
    conv_hbm,
    gain_one_hbm,
    gain_two_hbm,
    w_qkv_ref,
    bias_hbm,
    w_out_ref,
    w_up_ref,
    w_down_ref,
    out_ref,
    wide,
    normed,
    mixed,
    q_t,
    k_s,
    v_t,
    att_t,
    bias_s,
    w_qt,
    w_vt,
    score_s,
    prob_s,
    top_s,
    sum_s,
    held,
    w_qkv,
    w_out,
    w_up,
    w_down,
    conv_ref,
    gain_one_ref,
    gain_two_ref,
    bias_ref,
    load_sem,
    send_sem,
    recv_sem,
):
    columns, lat, width, heads, window, ff = dims
    radius = (window - 1) // 2
    reach = radius + 1
    keys = columns + 2 * radius
    head = width // heads
    tile = 128 // lat
    span = (columns + 2 * radius - tile) * lat
    pairs = heads // 2
    near = reach - tile
    groups = keys // tile
    axis = lax.axis_size("lon")
    me = lax.axis_index("lon")
    east, west = lax.rem(me + 1, axis), lax.rem(me + axis - 1, axis)
    core = lax.rem(me, 2)
    odd = jnp.where(me == 1, 0, core)

    barrier = pltpu.get_barrier_semaphore()
    for neighbour in (west, east):
        pl.semaphore_signal(
            barrier, inc=1, device_id={"lon": neighbour}, device_id_type=pl.DeviceIdType.MESH
        )
    loads = [
        pltpu.make_async_copy(tok_ref, wide.at[reach : reach + columns], load_sem.at[0]),
        pltpu.make_async_copy(w_qkv_ref, w_qkv, load_sem.at[1]),
        pltpu.make_async_copy(w_out_ref, w_out, load_sem.at[2]),
        pltpu.make_async_copy(w_up_ref, w_up, load_sem.at[3]),
        pltpu.make_async_copy(w_down_ref, w_down, load_sem.at[4]),
        pltpu.make_async_copy(conv_hbm, conv_ref, load_sem.at[5]),
        pltpu.make_async_copy(gain_one_hbm, gain_one_ref, load_sem.at[6]),
        pltpu.make_async_copy(gain_two_hbm, gain_two_ref, load_sem.at[7]),
        pltpu.make_async_copy(bias_hbm, bias_ref, load_sem.at[8]),
    ]
    for at in (8, 0, 5, 6, 7, 1, 2, 3, 4):
        loads[at].start()
    spans = (
        (east, columns - near, reach - near, near),
        (west, 0, reach + columns, near),
        (east, columns - reach, 0, reach - near),
        (west, near, reach + columns + near, reach - near),
    )
    sends = [
        pltpu.make_async_remote_copy(
            src_ref=tok_ref.at[source : source + size],
            dst_ref=wide.at[target : target + size],
            send_sem=send_sem.at[at],
            recv_sem=recv_sem.at[at],
            device_id={"lon": who},
            device_id_type=pl.DeviceIdType.MESH,
        )
        for at, (who, source, target, size) in enumerate(spans)
    ]
    first = me == 0
    second = jnp.logical_and(core == 1, me != axis - 1)

    def exchange(now):
        @pl.when(now)
        def _():
            pl.semaphore_wait(barrier, 2)
            for send in sends:
                send.start()

    exchange(jnp.logical_not(jnp.logical_or(first, second)))

    def arrive(far, side):
        start = side * (columns + reach + (0 if not far else near)) + (1 - side) * (
            0 if far else reach - near
        )
        size = reach - near if far else near
        pltpu.make_async_remote_copy(
            src_ref=tok_ref.at[0:size],
            dst_ref=wide.at[pl.ds(start, size)],
            send_sem=send_sem.at[2 * far + side],
            recv_sem=recv_sem.at[2 * far + side],
            device_id={"lon": east},
            device_id_type=pl.DeviceIdType.MESH,
        ).wait_recv()

    offsets = 2 * window - 1
    loads[8].wait()
    row = lax.broadcasted_iota(jnp.int32, (128, 128), 0)
    lane = lax.broadcasted_iota(jnp.int32, (128, 128), 1)
    flip = ((lane == (window - 1 - row + 128) % 128) & (row < offsets)).astype(F32)
    turned = []
    for b in range(window):
        piece = jnp.concatenate([bias_ref[b], jnp.zeros((heads, 128 - offsets), F32)], axis=1)
        turned.append(
            jnp.dot(
                piece, flip, preferred_element_type=F32, precision=lax.Precision.HIGHEST
            )
            * LOG2E
        )
    key_row = lax.broadcasted_iota(jnp.int32, (lat, 128), 0)
    lane = lax.broadcasted_iota(jnp.int32, (lat, 128), 1)
    lane_column = lane // lat
    start = jnp.clip(lane % lat - radius, 0, lat - window)
    inside = (key_row >= start) & (key_row < start + window)
    for kk in range(span // lat):
        line = jnp.zeros((heads, 128), F32)
        for cc in range(tile):
            if 0 <= kk - cc < window:
                line = line + pltpu.roll(turned[kk - cc], cc * lat, 1)
        valid = inside & (lane_column <= kk) & (lane_column > kk - window)
        for h in range(heads):
            spread = jnp.broadcast_to(line[h : h + 1], (lat, 128))
            rolled = pltpu.roll(spread, 0, 1, stride=1, stride_axis=0)
            bias_s[h // 2, kk * lat : (kk + 1) * lat, (h % 2) * 128 : (h % 2 + 1) * 128] = (
                jnp.where(valid, rolled, MASKED)
            )

    exchange(second)
    rows = lax.broadcasted_iota(jnp.int32, (lat, width), 0)

    def mix(first, count):
        gain_one = gain_one_ref[...]
        taps = [conv_ref[r + odd * (2 - 2 * r)] for r in range(3)]
        taps[1] = taps[1] + (lax.broadcasted_iota(jnp.int32, (3, width), 0) == 1).astype(F32)

        def fetch(u):
            return wide[u + odd * (keys + 1 - 2 * u)].astype(F32)

        x = [fetch(first), fetch(first + 1)]
        for m in range(first, first + count):
            j = m + odd * (keys - 1 - 2 * m)
            x = x[-2:] + [fetch(m + 2)]
            y = [
                taps[0][q : q + 1] * x[0] + taps[1][q : q + 1] * x[1] + taps[2][q : q + 1] * x[2]
                for q in range(3)
            ]
            above = pltpu.roll(y[0], 1, 0)
            above = jnp.concatenate([jnp.where(rows[:8] == 0, 0.0, above[:8]), above[8:]], axis=0)
            below = pltpu.roll(y[2], lat - 1, 0)
            below = jnp.concatenate(
                [below[: lat - 8], jnp.where(rows[lat - 8 :] == lat - 1, 0.0, below[lat - 8 :])], axis=0
            )
            total = (y[1] + (above + below)).astype(BF16)
            mixed[j] = total
            normed[j] = norm(total.astype(F32), gain_one)

    def project(m):
        g = m + odd * (groups - 1 - 2 * m)
        flat = normed[pl.ds(g * tile, tile)].reshape(128, width)
        at = pl.ds(pl.multiple_of(g * 128, 128), 128)
        k_s[at] = jnp.dot(
            flat, w_qkv[:, width : 2 * width], preferred_element_type=F32
        ).astype(BF16)
        v_t[:, at] = lax.dot_general(
            w_vt[...], flat, (((1,), (1,)), ((), ())), preferred_element_type=F32
        ).astype(BF16)

    scale = LOG2E / float(head) ** 0.5

    def tile_of(late):
        return odd if late else 1 - odd

    def query(late):
        first = radius + tile_of(late) * tile
        q_t[late] = (
            lax.dot_general(
                w_qt[...],
                normed[pl.ds(first, tile)].reshape(128, width),
                (((1,), (1,)), ((), ())),
                preferred_element_type=F32,
            )
            * scale
        ).astype(BF16)

    blank = jnp.zeros((head, 128), BF16)
    early = span - 128
    slots = 8

    def place(block):
        late, part, pair = block
        size = 128 if part else early
        off = odd * early if part else (1 - odd) * 128
        there = pl.ds(pl.multiple_of(tile_of(late) * 128 + off, 128), size)
        return size, pl.ds(pl.multiple_of(off, 128), size), there, slice(pair * 2 * head, (pair + 1) * 2 * head)

    def score(step, block):
        late, part, pair = block
        size, off, there, at = place(block)
        q_a = q_t[late, pair * 2 * head : pair * 2 * head + head]
        q_b = q_t[late, pair * 2 * head + head : (pair + 1) * 2 * head]
        q_two = jnp.concatenate(
            [jnp.concatenate([q_a, blank], axis=1), jnp.concatenate([blank, q_b], axis=1)],
            axis=0,
        )
        scores = jnp.dot(k_s[there, at], q_two, preferred_element_type=F32) + bias_s[pair, off]
        score_s[step % slots, :size] = scores
        top = jnp.max(scores, axis=0, keepdims=True)
        if part:
            top = jnp.maximum(top, top_s[late, pair])
        else:
            top_s[late, pair] = top
        return top

    def soften(step, block, top):
        size = place(block)[0]
        prob_s[step % slots, :size] = jnp.exp2((score_s[step % slots, :size] - top).astype(BF16))

    def gather(step, block, top):
        late, part, pair = block
        size, _, there, at = place(block)
        o = jnp.dot(v_t[at, there], prob_s[step % slots, :size], preferred_element_type=F32)
        total = jnp.dot(
            jnp.ones((16, size), BF16), prob_s[step % slots, :size], preferred_element_type=F32
        )[:1]
        o_a, o_b = o[:head, :128], o[head:, 128:]
        if part:
            keep = jnp.exp2(top_s[late, pair] - top)
            scaled = 1.0 / (total + keep * sum_s[late, pair])
            keep = keep * scaled
            o_a = o_a * scaled[:, :128] + held[late, pair, :head] * keep[:, :128]
            o_b = o_b * scaled[:, 128:] + held[late, pair, head:] * keep[:, 128:]
            att_t[tile_of(late), at] = jnp.concatenate([o_a, o_b], axis=0).astype(BF16)
        else:
            sum_s[late, pair] = total
            held[late, pair] = jnp.concatenate([o_a, o_b], axis=0)

    def attend(blocks, apart=3):
        tops = {}
        for step in range(len(blocks) + 2 * apart):
            if step < len(blocks):
                tops[step] = score(step, blocks[step])
            at = step - apart
            if 0 <= at < len(blocks):
                soften(at, blocks[at], tops[at])
            at = step - 2 * apart
            if 0 <= at < len(blocks):
                gather(at, blocks[at], tops[at])

    for at in (0, 5, 6, 7):
        loads[at].wait()
    mix(reach, columns - 2)
    loads[1].wait()
    w_qt[...] = w_qkv[:, :width].T
    w_vt[...] = w_qkv[:, 2 * width : 3 * width].T
    project(2)
    arrive(0, 1 - odd)
    mix(keys - reach, near)
    project(3)
    query(0)
    exchange(first)
    arrive(1, 1 - odd)
    mix(keys - tile, tile)
    project(4)
    attend([(0, 0, pair) for pair in range(pairs)])
    arrive(0, odd)
    mix(tile, near)
    query(1)
    project(1)
    attend([(0, 1, pair) for pair in range(pairs)] + [(1, 0, pair) for pair in range(pairs)])
    for at in (2, 3, 4):
        loads[at].wait()
    arrive(1, odd)
    mix(0, tile)
    project(0)
    attend([(1, 1, pair) for pair in range(pairs)])

    flat_in = mixed[radius : radius + columns].reshape(columns * lat, width)
    attended = jnp.concatenate([att_t[t] for t in range(columns // tile)], axis=1)
    stream = (
        flat_in.astype(F32) + lax.dot_general(
            attended, w_out[...], (((0,), (0,)), ((), ())), preferred_element_type=F32
        )
    ).astype(BF16)
    normed_two = norm(stream.astype(F32), gain_two_ref[...])
    total = stream.astype(F32)
    chunk = 1024

    def raise_(at):
        return jnp.dot(normed_two, w_up[:, at : at + chunk], preferred_element_type=F32)

    ahead = raise_(0)
    for at in range(0, ff, chunk):
        now = ahead
        if at + chunk < ff:
            ahead = raise_(at + chunk)
        hidden = gelu(now.astype(BF16))
        total = total + jnp.dot(hidden, w_down[at : at + chunk], preferred_element_type=F32)
    out_ref[...] = total.astype(BF16).reshape(columns, lat, width)
    for send in sends:
        send.wait_send()


def on_device(tokens, conv_weight, gain_one, gain_two, w_qkv, rel_bias, w_out, w_up, w_down):
    columns, lat, width = tokens.shape
    heads, _, window = rel_bias.shape
    ff = w_up.shape[1]
    radius = (window - 1) // 2
    keys = columns + 2 * radius
    dims = (columns, lat, width, heads, window, ff)
    vmem = pl.BlockSpec(memory_space=pltpu.VMEM)
    hbm = pl.BlockSpec(memory_space=pltpu.MemorySpace.HBM)
    return pl.pallas_call(
        functools.partial(block_kernel, dims),
        out_shape=pltpu.VMEM(tokens.shape, BF16),
        in_specs=[hbm] * 9,
        out_specs=vmem,
        scratch_shapes=[
            pltpu.VMEM((keys + 2, lat, width), BF16),
            pltpu.VMEM((keys, lat, width), BF16),
            pltpu.VMEM((keys, lat, width), BF16),
            pltpu.VMEM((2, width, 128), BF16),
            pltpu.VMEM((keys * lat, width), BF16),
            pltpu.VMEM((width, keys * lat), BF16),
            pltpu.VMEM((2, width, 128), BF16),
            pltpu.VMEM((heads // 2, keys * lat - 128, 256), F32),
            pltpu.VMEM((width, width), BF16),
            pltpu.VMEM((width, width), BF16),
            pltpu.VMEM((8, keys * lat - 256, 256), F32),
            pltpu.VMEM((8, keys * lat - 256, 256), BF16),
            pltpu.VMEM((2, heads // 2, 1, 256), F32),
            pltpu.VMEM((2, heads // 2, 1, 256), F32),
            pltpu.VMEM((2, heads // 2, 2 * width // heads, 128), F32),
            pltpu.VMEM(w_qkv.shape, BF16),
            pltpu.VMEM(w_out.shape, BF16),
            pltpu.VMEM(w_up.shape, BF16),
            pltpu.VMEM(w_down.shape, BF16),
            pltpu.VMEM(conv_weight.shape, F32),
            pltpu.VMEM((1, width), F32),
            pltpu.VMEM((1, width), F32),
            pltpu.VMEM((window, heads, rel_bias.shape[1]), F32),
            pltpu.SemaphoreType.DMA((9,)),
            pltpu.SemaphoreType.DMA((4,)),
            pltpu.SemaphoreType.DMA((4,)),
        ],
        compiler_params=pltpu.CompilerParams(
            collective_id=0, has_side_effects=True, vmem_limit_bytes=64 * 1024 * 1024 - 327680
        ),
    )(
        tokens,
        conv_weight,
        gain_one.reshape(1, width),
        gain_two.reshape(1, width),
        w_qkv,
        jnp.transpose(rel_bias, (2, 0, 1)),
        w_out,
        w_up,
        w_down,
    )


def solution(mesh):
    placed = (P(("grp", "lon"), None, None), P(), P(), P(), P(), P(), P(), P(), P())
    return jax.shard_map(
        on_device,
        mesh=mesh,
        in_specs=placed,
        out_specs=P(("grp", "lon"), None, None),
        check_vma=False,
    )
```

```python
import functools

import jax
import jax.numpy as jnp
from jax import lax
from jax.experimental import pallas as pl
from jax.experimental.pallas import tpu as pltpu
from jax.sharding import PartitionSpec as P

EPS = 1e-05
LOG2E = 1.4426950408889634
F32 = jnp.float32
BF16 = jnp.bfloat16
MASKED = -1e30


def norm(values, gain):
    center = values - jnp.mean(values, axis=-1, keepdims=True)
    spread = jnp.mean(center * center, axis=-1, keepdims=True)
    return (center * lax.rsqrt(spread + EPS) * gain).astype(BF16)


def gelu(x):
    half = x * BF16(0.5)
    inner = x * (BF16(0.7978845608028654) + BF16(0.035677408136300125) * (x * x))
    return half + half * jnp.tanh(inner)


def block_kernel(
    dims,
    tok_ref,
    conv_hbm,
    gain_one_hbm,
    gain_two_hbm,
    w_qkv_ref,
    bias_hbm,
    w_out_ref,
    w_up_ref,
    w_down_ref,
    out_ref,
    wide,
    normed,
    mixed,
    q_t,
    k_s,
    v_t,
    att_t,
    bias_s,
    w_qt,
    score_s,
    prob_s,
    top_s,
    sum_s,
    held,
    w_qkv,
    w_out,
    w_up,
    w_down,
    conv_ref,
    gain_one_ref,
    gain_two_ref,
    bias_ref,
    load_sem,
    send_sem,
    recv_sem,
):
    columns, lat, width, heads, window, ff = dims
    radius = (window - 1) // 2
    reach = radius + 1
    keys = columns + 2 * radius
    head = width // heads
    tile = 128 // lat
    span = (columns + 2 * radius - tile) * lat
    pairs = heads // 2
    near = reach - tile
    groups = keys // tile
    axis = lax.axis_size("lon")
    me = lax.axis_index("lon")
    east, west = lax.rem(me + 1, axis), lax.rem(me + axis - 1, axis)
    core = lax.rem(me, 2)
    odd = jnp.where(me == 1, 0, core)

    barrier = pltpu.get_barrier_semaphore()
    for neighbour in (west, east):
        pl.semaphore_signal(
            barrier, inc=1, device_id={"lon": neighbour}, device_id_type=pl.DeviceIdType.MESH
        )
    loads = [
        pltpu.make_async_copy(tok_ref, wide.at[reach : reach + columns], load_sem.at[0]),
        pltpu.make_async_copy(w_qkv_ref, w_qkv, load_sem.at[1]),
        pltpu.make_async_copy(w_out_ref, w_out, load_sem.at[2]),
        pltpu.make_async_copy(w_up_ref, w_up, load_sem.at[3]),
        pltpu.make_async_copy(w_down_ref, w_down, load_sem.at[4]),
        pltpu.make_async_copy(conv_hbm, conv_ref, load_sem.at[5]),
        pltpu.make_async_copy(gain_one_hbm, gain_one_ref, load_sem.at[6]),
        pltpu.make_async_copy(gain_two_hbm, gain_two_ref, load_sem.at[7]),
        pltpu.make_async_copy(bias_hbm, bias_ref, load_sem.at[8]),
    ]
    for at in (8, 0, 5, 6, 7, 1, 2, 3, 4):
        loads[at].start()
    spans = (
        (east, columns - near, reach - near, near),
        (west, 0, reach + columns, near),
        (east, columns - reach, 0, reach - near),
        (west, near, reach + columns + near, reach - near),
    )
    sends = [
        pltpu.make_async_remote_copy(
            src_ref=tok_ref.at[source : source + size],
            dst_ref=wide.at[target : target + size],
            send_sem=send_sem.at[at],
            recv_sem=recv_sem.at[at],
            device_id={"lon": who},
            device_id_type=pl.DeviceIdType.MESH,
        )
        for at, (who, source, target, size) in enumerate(spans)
    ]
    first = me == 0
    second = jnp.logical_and(core == 1, me != axis - 1)

    def exchange(now):
        @pl.when(now)
        def _():
            pl.semaphore_wait(barrier, 2)
            for send in sends:
                send.start()

    exchange(jnp.logical_not(jnp.logical_or(first, second)))

    def arrive(far, side):
        start = side * (columns + reach + (0 if not far else near)) + (1 - side) * (
            0 if far else reach - near
        )
        size = reach - near if far else near
        pltpu.make_async_remote_copy(
            src_ref=tok_ref.at[0:size],
            dst_ref=wide.at[pl.ds(start, size)],
            send_sem=send_sem.at[2 * far + side],
            recv_sem=recv_sem.at[2 * far + side],
            device_id={"lon": east},
            device_id_type=pl.DeviceIdType.MESH,
        ).wait_recv()

    offsets = 2 * window - 1
    loads[8].wait()
    row = lax.broadcasted_iota(jnp.int32, (128, 128), 0)
    lane = lax.broadcasted_iota(jnp.int32, (128, 128), 1)
    flip = ((lane == (window - 1 - row + 128) % 128) & (row < offsets)).astype(F32)
    turned = []
    for b in range(window):
        piece = jnp.concatenate([bias_ref[b], jnp.zeros((heads, 128 - offsets), F32)], axis=1)
        turned.append(
            jnp.dot(
                piece, flip, preferred_element_type=F32, precision=lax.Precision.HIGHEST
            )
            * LOG2E
        )
    key_row = lax.broadcasted_iota(jnp.int32, (lat, 128), 0)
    lane = lax.broadcasted_iota(jnp.int32, (lat, 128), 1)
    lane_column = lane // lat
    start = jnp.clip(lane % lat - radius, 0, lat - window)
    inside = (key_row >= start) & (key_row < start + window)
    for kk in range(span // lat):
        line = jnp.zeros((heads, 128), F32)
        for cc in range(tile):
            if 0 <= kk - cc < window:
                line = line + pltpu.roll(turned[kk - cc], cc * lat, 1)
        valid = inside & (lane_column <= kk) & (lane_column > kk - window)
        for h in range(heads):
            spread = jnp.broadcast_to(line[h : h + 1], (lat, 128))
            rolled = pltpu.roll(spread, 0, 1, stride=1, stride_axis=0)
            bias_s[h // 2, kk * lat : (kk + 1) * lat, (h % 2) * 128 : (h % 2 + 1) * 128] = (
                jnp.where(valid, rolled, MASKED)
            )

    exchange(second)
    rows = lax.broadcasted_iota(jnp.int32, (lat, width), 0)

    def mix(first, count):
        gain_one = gain_one_ref[...]
        taps = [conv_ref[r + odd * (2 - 2 * r)] for r in range(3)]
        taps[1] = taps[1] + (lax.broadcasted_iota(jnp.int32, (3, width), 0) == 1).astype(F32)

        def fetch(u):
            return wide[u + odd * (keys + 1 - 2 * u)].astype(F32)

        x = [fetch(first), fetch(first + 1)]
        for m in range(first, first + count):
            j = m + odd * (keys - 1 - 2 * m)
            x = x[-2:] + [fetch(m + 2)]
            y = [
                taps[0][q : q + 1] * x[0] + taps[1][q : q + 1] * x[1] + taps[2][q : q + 1] * x[2]
                for q in range(3)
            ]
            above = pltpu.roll(y[0], 1, 0)
            above = jnp.concatenate([jnp.where(rows[:8] == 0, 0.0, above[:8]), above[8:]], axis=0)
            below = pltpu.roll(y[2], lat - 1, 0)
            below = jnp.concatenate(
                [below[: lat - 8], jnp.where(rows[lat - 8 :] == lat - 1, 0.0, below[lat - 8 :])], axis=0
            )
            total = (y[1] + (above + below)).astype(BF16)
            mixed[j] = total
            normed[j] = norm(total.astype(F32), gain_one)

    def project(m):
        g = m + odd * (groups - 1 - 2 * m)
        flat = normed[pl.ds(g * tile, tile)].reshape(128, width)
        at = pl.ds(pl.multiple_of(g * 128, 128), 128)
        k_s[at] = jnp.dot(
            flat, w_qkv[:, width : 2 * width], preferred_element_type=F32
        ).astype(BF16)
        v_t[:, at] = jnp.dot(
            flat, w_qkv[:, 2 * width : 3 * width], preferred_element_type=F32
        ).astype(BF16).T

    scale = LOG2E / float(head) ** 0.5

    def tile_of(late):
        return odd if late else 1 - odd

    def query(late):
        first = radius + tile_of(late) * tile
        q_t[late] = (
            lax.dot_general(
                w_qt[...],
                normed[pl.ds(first, tile)].reshape(128, width),
                (((1,), (1,)), ((), ())),
                preferred_element_type=F32,
            )
            * scale
        ).astype(BF16)

    blank = jnp.zeros((head, 128), BF16)
    early = span - 128
    slots = 8

    def place(block):
        late, part, pair = block
        size = 128 if part else early
        off = odd * early if part else (1 - odd) * 128
        there = pl.ds(pl.multiple_of(tile_of(late) * 128 + off, 128), size)
        return size, pl.ds(pl.multiple_of(off, 128), size), there, slice(pair * 2 * head, (pair + 1) * 2 * head)

    def score(step, block):
        late, part, pair = block
        size, off, there, at = place(block)
        q_a = q_t[late, pair * 2 * head : pair * 2 * head + head]
        q_b = q_t[late, pair * 2 * head + head : (pair + 1) * 2 * head]
        q_two = jnp.concatenate(
            [jnp.concatenate([q_a, blank], axis=1), jnp.concatenate([blank, q_b], axis=1)],
            axis=0,
        )
        scores = jnp.dot(k_s[there, at], q_two, preferred_element_type=F32) + bias_s[pair, off]
        score_s[step % slots, :size] = scores
        top = jnp.max(scores, axis=0, keepdims=True)
        if part:
            top = jnp.maximum(top, top_s[late, pair])
        else:
            top_s[late, pair] = top
        return top

    def soften(step, block, top):
        size = place(block)[0]
        prob_s[step % slots, :size] = jnp.exp2((score_s[step % slots, :size] - top).astype(BF16))

    def gather(step, block, top):
        late, part, pair = block
        size, _, there, at = place(block)
        o = jnp.dot(v_t[at, there], prob_s[step % slots, :size], preferred_element_type=F32)
        total = jnp.dot(
            jnp.ones((16, size), BF16), prob_s[step % slots, :size], preferred_element_type=F32
        )[:1]
        o_a, o_b = o[:head, :128], o[head:, 128:]
        if part:
            keep = jnp.exp2(top_s[late, pair] - top)
            scaled = 1.0 / (total + keep * sum_s[late, pair])
            keep = keep * scaled
            o_a = o_a * scaled[:, :128] + held[late, pair, :head] * keep[:, :128]
            o_b = o_b * scaled[:, 128:] + held[late, pair, head:] * keep[:, 128:]
            att_t[tile_of(late), at] = jnp.concatenate([o_a, o_b], axis=0).astype(BF16)
        else:
            sum_s[late, pair] = total
            held[late, pair] = jnp.concatenate([o_a, o_b], axis=0)

    def attend(blocks, apart=3):
        tops = {}
        for step in range(len(blocks) + 2 * apart):
            if step < len(blocks):
                tops[step] = score(step, blocks[step])
            at = step - apart
            if 0 <= at < len(blocks):
                soften(at, blocks[at], tops[at])
            at = step - 2 * apart
            if 0 <= at < len(blocks):
                gather(at, blocks[at], tops[at])

    for at in (0, 5, 6, 7):
        loads[at].wait()
    mix(reach, columns - 2)
    loads[1].wait()
    w_qt[...] = w_qkv[:, :width].T
    project(2)
    arrive(0, 1 - odd)
    mix(keys - reach, near)
    project(3)
    query(0)
    exchange(first)
    arrive(1, 1 - odd)
    mix(keys - tile, tile)
    project(4)
    attend([(0, 0, pair) for pair in range(pairs)])
    arrive(0, odd)
    mix(tile, near)
    query(1)
    project(1)
    attend([(0, 1, pair) for pair in range(pairs)] + [(1, 0, pair) for pair in range(pairs)])
    for at in (2, 3, 4):
        loads[at].wait()
    arrive(1, odd)
    mix(0, tile)
    project(0)
    attend([(1, 1, pair) for pair in range(pairs)])

    flat_in = mixed[radius : radius + columns].reshape(columns * lat, width)
    attended = jnp.concatenate([att_t[t] for t in range(columns // tile)], axis=1)
    stream = (
        flat_in.astype(F32) + lax.dot_general(
            attended, w_out[...], (((0,), (0,)), ((), ())), preferred_element_type=F32
        )
    ).astype(BF16)
    normed_two = norm(stream.astype(F32), gain_two_ref[...])
    total = stream.astype(F32)
    chunk = 1024

    def raise_(at):
        return jnp.dot(normed_two, w_up[:, at : at + chunk], preferred_element_type=F32)

    ahead = raise_(0)
    for at in range(0, ff, chunk):
        now = ahead
        if at + chunk < ff:
            ahead = raise_(at + chunk)
        hidden = gelu(now.astype(BF16))
        total = total + jnp.dot(hidden, w_down[at : at + chunk], preferred_element_type=F32)
    out_ref[...] = total.astype(BF16).reshape(columns, lat, width)
    for send in sends:
        send.wait_send()


def on_device(tokens, conv_weight, gain_one, gain_two, w_qkv, rel_bias, w_out, w_up, w_down):
    columns, lat, width = tokens.shape
    heads, _, window = rel_bias.shape
    ff = w_up.shape[1]
    radius = (window - 1) // 2
    keys = columns + 2 * radius
    dims = (columns, lat, width, heads, window, ff)
    vmem = pl.BlockSpec(memory_space=pltpu.VMEM)
    hbm = pl.BlockSpec(memory_space=pltpu.MemorySpace.HBM)
    return pl.pallas_call(
        functools.partial(block_kernel, dims),
        out_shape=pltpu.VMEM(tokens.shape, BF16),
        in_specs=[hbm] * 9,
        out_specs=vmem,
        scratch_shapes=[
            pltpu.VMEM((keys + 2, lat, width), BF16),
            pltpu.VMEM((keys, lat, width), BF16),
            pltpu.VMEM((keys, lat, width), BF16),
            pltpu.VMEM((2, width, 128), BF16),
            pltpu.VMEM((keys * lat, width), BF16),
            pltpu.VMEM((width, keys * lat), BF16),
            pltpu.VMEM((2, width, 128), BF16),
            pltpu.VMEM((heads // 2, keys * lat - 128, 256), F32),
            pltpu.VMEM((width, width), BF16),
            pltpu.VMEM((8, keys * lat - 256, 256), F32),
            pltpu.VMEM((8, keys * lat - 256, 256), BF16),
            pltpu.VMEM((2, heads // 2, 1, 256), F32),
            pltpu.VMEM((2, heads // 2, 1, 256), F32),
            pltpu.VMEM((2, heads // 2, 2 * width // heads, 128), F32),
            pltpu.VMEM(w_qkv.shape, BF16),
            pltpu.VMEM(w_out.shape, BF16),
            pltpu.VMEM(w_up.shape, BF16),
            pltpu.VMEM(w_down.shape, BF16),
            pltpu.VMEM(conv_weight.shape, F32),
            pltpu.VMEM((1, width), F32),
            pltpu.VMEM((1, width), F32),
            pltpu.VMEM((window, heads, rel_bias.shape[1]), F32),
            pltpu.SemaphoreType.DMA((9,)),
            pltpu.SemaphoreType.DMA((4,)),
            pltpu.SemaphoreType.DMA((4,)),
        ],
        compiler_params=pltpu.CompilerParams(
            collective_id=0, has_side_effects=True, vmem_limit_bytes=64 * 1024 * 1024 - 327680
        ),
    )(
        tokens,
        conv_weight,
        gain_one.reshape(1, width),
        gain_two.reshape(1, width),
        w_qkv,
        jnp.transpose(rel_bias, (2, 0, 1)),
        w_out,
        w_up,
        w_down,
    )


def solution(mesh):
    placed = (P(("grp", "lon"), None, None), P(), P(), P(), P(), P(), P(), P(), P())
    return jax.shard_map(
        on_device,
        mesh=mesh,
        in_specs=placed,
        out_specs=P(("grp", "lon"), None, None),
        check_vma=False,
    )
```
